32 devices in a mesh: section: 8 (over z, x), fsdp: 4 (over y, core).
Axes of the slice: x: 2, y: 2, z: 4, core: 2. Of those that a mesh axis runs over, the one named last changes fastest.
Arguments:
- hidden: bfloat16 [2, 8, 512, 256], P(None, 'section', 'fsdp'), may hold values from -6 to 6
- grad_out: bfloat16 [2, 8, 512, 4096], P(None, 'section', 'fsdp'), may hold values from -0.375 to 0.375
- live_cols: int32 [8], replicated, may hold values from 128 to 256, as said below
- tok_count: int32 [2, 4], P(None, 'fsdp'), may hold values from 1 to 128, 384 in all within a row
Outputs:
- grad_down_t: float32 [8, 4096, 256], P('section', 'fsdp')
The draws below stay inside these ranges and needn't reach their ends.
Inputs may be any that keep to these rules, and one draw needn't show every extreme that they name: `live_cols`: each entry is a multiple of 128; some section has all 256 hidden units live. `tok_count`: each direction's counts sum to 384, and some device of each direction holds 128 live tokens.
All inputs are finite; a program needn't handle non-finite values.
Results may differ from the reference program's by a relative error of at most 0.0003.
Values sent between devices are 32-bit elements; how exact they have to be, the bound alone decides.
A program may use at most 64 MiB of HBM per device.

```python
import math
import jax
import jax.numpy as jnp
import numpy as np
from jax import lax

D = 4096
BLK = 128
NBLK = 2
HID = 256
TOK = 128
TOKENS = 512
N_SECTION = 8
N_FSDP = 4


def draw_live_cols(key, part):
    first_key, second_key = jax.random.split(jax.random.fold_in(key, 17))
    blocks_live = jax.random.randint(first_key, (N_SECTION,), 1, NBLK + 1)
    fullest = jax.random.randint(second_key, (), 0, N_SECTION)
    blocks_live = blocks_live.at[fullest].set(NBLK)
    return (blocks_live * BLK).astype(jnp.int32)


def with_spikes(values, key, source, target, blocks, factor):
    owner, partner = [(jnp.arange(values.shape[dim]) // (values.shape[dim] // blocks)).reshape([-1 if axis == dim else 1 for axis in range(values.ndim)]) for dim in (source, target)]
    chosen = jax.random.permutation(key, blocks)[partner]
    strong = (owner == chosen) | (owner == (partner + blocks // 2) % blocks)
    return jnp.where(strong, factor * values, values)


def steps_of(rng, extent, pieces, low, top_value):
    def one(position, blocks):
        heights = jax.random.uniform(jax.random.fold_in(jax.random.fold_in(rng, 6), position), (blocks,), jnp.float32, low / len(pieces), top_value / len(pieces))
        return jnp.repeat(jnp.exp(heights), extent[position] // blocks).reshape((-1,) + (1,) * (len(extent) - position - 1))

    gain = one(*pieces[0])
    for cut in pieces[1:]:
        gain = gain * one(*cut)
    return gain


def length_profile(number_of, total, reach, lean):
    weights = [(1 << 20) // math.isqrt(grade ** lean) + 1 for grade in range(2, number_of + 1)]
    rest, holding = total - reach - (number_of - 1), [1] * (number_of - 1)
    while rest > 0:
        movable = [i for i in range(number_of - 1) if holding[i] < reach]
        mass, left = sum([weights[i] for i in movable]), rest
        for i in movable:
            addition = min(reach - holding[i], max(1, left * weights[i] // mass), rest)
            holding[i] = holding[i] + addition
            rest = rest - addition
    return np.array([reach] + holding)


def ragged(stream_key, count, total, limit, skew):
    if count == 2:
        one = jax.random.randint(stream_key, (), max(1, total - limit), min(limit, total - 1) + 1)
        return jnp.stack([one, total - one])
    lengths = jnp.asarray(length_profile(count, total, limit, skew), jnp.int32)
    couples = (count - 1) // 2
    giver, sink = lengths[1:1 + 2 * couples:2], lengths[2:2 + 2 * couples:2]
    margin = jnp.minimum(giver - 1, limit - sink)
    passed = jax.random.randint(jax.random.fold_in(stream_key, 1), (couples,), 0, 1 << 20) % (margin + 1)
    lengths = lengths.at[1:1 + 2 * couples:2].set(giver - passed).at[2:2 + 2 * couples:2].set(sink + passed)
    return lengths[jax.random.permutation(jax.random.fold_in(stream_key, 2), count)]


def centred(rng, extent, width, bound, cuts=(), kind=jnp.bfloat16):
    result = width * jax.random.normal(rng, extent, jnp.float32)
    if cuts:
        result = result * steps_of(rng, extent, cuts, -0.22, 0.18)
    return jnp.clip(result, -bound, bound).astype(kind)


def heavy_noise(own_key, dims, deviation, bound, cuts, heavy, kind=jnp.bfloat16):
    entries = deviation * jax.random.normal(own_key, dims, jnp.float32)
    if cuts:
        entries = entries * steps_of(own_key, dims, cuts, -0.22, 0.18)
    return jnp.clip(with_spikes(entries, jax.random.fold_in(own_key, 3), *heavy), -bound, bound).astype(kind)


def setup_inputs(seed: int = 0) -> dict:
    streams_of = jax.random.split(jax.random.key(seed), 5)
    hidden = centred(streams_of[0], (2, N_SECTION, TOKENS, HID), 1.0, 6.0, ((1, 8), (2, 4)))
    grad_out = heavy_noise(streams_of[1], (2, N_SECTION, TOKENS, D), ((TOK * N_FSDP) ** -0.5), 0.375, ((1, 8), (2, 4)), (2, 3, 4, 2.0))
    live_cols = draw_live_cols(jax.random.fold_in(streams_of[4], 71), 0)
    tok_count = jax.vmap(lambda own: ragged(own, N_FSDP, TOKENS * 3 // 4, TOK, 1))(jax.random.split(streams_of[3], 2)).reshape((2, N_FSDP)).astype(jnp.int32)
    return {"hidden": hidden, "grad_out": grad_out, "live_cols": live_cols, "tok_count": tok_count}


def one_layer(hidden_rows, grad_rows, live_count, counts):
    positions = jnp.arange(TOKENS, dtype=jnp.int32) % TOK
    owners = jnp.arange(TOKENS, dtype=jnp.int32) // TOK
    limits = counts[owners]
    column_ids = jnp.arange(HID, dtype=jnp.int32)
    keep_mask = (positions < limits)[:, None] & (column_ids < live_count)[None, :]
    masked = jnp.where(keep_mask, hidden_rows, jnp.zeros_like(hidden_rows))
    split_hidden = masked.reshape(N_FSDP, TOK, HID).astype(jnp.float32)
    split_grads = grad_rows.reshape(N_FSDP, TOK, D).astype(jnp.float32)
    partials = jnp.einsum("ftd,fth->fdh", split_grads, split_hidden)
    return jnp.sum(partials, axis=0)


def reference(hidden, grad_out, live_cols, tok_count):
    section_ids = jnp.arange(N_SECTION, dtype=jnp.int32)
    live_up = live_cols[(N_SECTION - 1 - section_ids).astype(jnp.int32)]

    def run_layer(items):
        hidden_rows, grad_rows, live_count, counts = items
        return one_layer(hidden_rows, grad_rows, live_count, counts)

    counts_down = jnp.broadcast_to(tok_count[0], (N_SECTION, N_FSDP))
    counts_up = jnp.broadcast_to(tok_count[1], (N_SECTION, N_FSDP))
    down_sums = lax.map(run_layer, (hidden[0], grad_out[0], live_cols, counts_down))
    up_sums = lax.map(run_layer, (hidden[1], grad_out[1], live_up, counts_up))
    return down_sums + up_sums[::-1]
```

```python
import functools

import jax
import jax.numpy as jnp
from jax import lax
from jax.experimental import pallas as pl
from jax.experimental.pallas import tpu as pltpu
from jax.sharding import PartitionSpec as P

MESH = pl.DeviceIdType.MESH


def kernel(
    sections, chips, chunk, hidden, grads, live_cols, tok_count, out,
    mask_send, mask_recv, in_send, in_recv, own_mask, part_send, part_recv, far_send, far_recv,
    mask_ss, mask_rs, in_ss, in_rs, part_ss, part_rs, far_ss, far_rs,
):
    tokens, width = hidden.shape[2], hidden.shape[3]
    rows = out.shape[1]
    chunks = rows // chunk
    sec = lax.axis_index("section")
    rank = lax.axis_index("fsdp")
    chip, core = rank // 2, rank % 2
    sibling = {"section": sec, "fsdp": chip * 2 + (1 - core)}
    mirrored = {"section": sections - 1 - sec, "fsdp": rank}

    def peer(j):
        return {"section": sec, "fsdp": lax.rem(chip + j, chips) * 2 + core}

    barrier = pltpu.get_barrier_semaphore()
    for target in [sibling, mirrored] + [peer(j) for j in range(1, chips)]:
        pl.semaphore_signal(barrier, inc=1, device_id=target, device_id_type=MESH)

    def columns(j, c, k):
        block = lax.rem(chip + j, chips) * 2 + c
        return pl.ds(pl.multiple_of(block * rows + k * chunk, chunk), chunk)

    def mask_copy(d):
        return pltpu.make_async_remote_copy(
            mask_send.at[d], mask_recv.at[d], mask_ss.at[d], mask_rs.at[d],
            device_id=sibling, device_id_type=MESH)

    def in_copy(d, j, k):
        return pltpu.make_async_remote_copy(
            in_send.at[d, j, k], in_recv.at[d, j, k], in_ss.at[d, j, k], in_rs.at[d, j, k],
            device_id=sibling, device_id_type=MESH)

    def part_copy(d, j, k):
        return pltpu.make_async_remote_copy(
            part_send.at[d, j - 1, k], part_recv.at[d, j - 1, k],
            part_ss.at[d, j - 1, k], part_rs.at[d, j - 1, k],
            device_id=peer(j), device_id_type=MESH)

    def far_copy(k):
        return pltpu.make_async_remote_copy(
            far_send.at[k], far_recv.at[k], far_ss.at[k], far_rs.at[k],
            device_id=mirrored, device_id_type=MESH)

    positions = lax.broadcasted_iota(jnp.int32, (tokens, width), 0)
    column_ids = lax.broadcasted_iota(jnp.int32, (tokens, width), 1)
    live = (live_cols[sec], live_cols[sections - 1 - sec])
    order = [(k, j) for k in range(chunks) for j in list(range(1, chips)) + [0]]

    first = True
    for d in (1, 0):
        keep = (positions < tok_count[d, 0]) & (column_ids < live[d])
        masked = jnp.where(keep, hidden[d, 0].astype(jnp.float32), 0.0)
        mask_send[d] = masked
        own_mask[d, :tokens] = masked.astype(jnp.bfloat16)
        for k, j in order:
            in_send[d, j, k] = grads[d, 0, :, columns(j, 1 - core, k)].astype(jnp.float32)
            if first:
                pl.semaphore_wait(barrier, chips + 1)
                first = False
                mask_copy(d).start()
            elif (k, j) == order[0]:
                mask_copy(d).start()
            in_copy(d, j, k).start()

    def partial(d, j, k):
        in_copy(d, j, k).wait_recv()
        both = jnp.concatenate(
            [grads[d, 0, :, columns(j, core, k)], in_recv[d, j, k].astype(jnp.bfloat16)], axis=0)
        return lax.dot_general(
            both, own_mask[d], (((0,), (0,)), ((), ())), preferred_element_type=jnp.float32)

    def take_mask(d):
        mask_copy(d).wait_recv()
        own_mask[d, tokens:] = mask_recv[d].astype(jnp.bfloat16)

    def send_parts(d, k):
        for j in range(1, chips):
            part_send[d, j - 1, k] = partial(d, j, k)
            part_copy(d, j, k).start()

    take_mask(1)
    for k in range(chunks):
        send_parts(1, k)
        far_send[k] = partial(1, 0, k)
    take_mask(0)
    for k in range(chunks):
        total = far_send[k]
        for j in range(1, chips):
            part_copy(1, j, k).wait_recv()
            total = total + part_recv[1, j - 1, k]
        far_send[k] = total
        far_copy(k).start()
        send_parts(0, k)
        out[0, k * chunk:(k + 1) * chunk] = partial(0, 0, k)
    for k in range(chunks):
        here = slice(k * chunk, (k + 1) * chunk)
        total = out[0, here]
        for j in range(1, chips):
            part_copy(0, j, k).wait_recv()
            total = total + part_recv[0, j - 1, k]
        far_copy(k).wait_recv()
        out[0, here] = total + far_recv[k]
    for d in (1, 0):
        mask_copy(d).wait_send()
        for k, j in order:
            in_copy(d, j, k).wait_send()
            if j:
                part_copy(d, j, k).wait_send()
    for k in range(chunks):
        far_copy(k).wait_send()


def on_device(sections, ranks, hidden, grad_out, live_cols, tok_count):
    tokens, width = hidden.shape[2], hidden.shape[3]
    rows = grad_out.shape[3] // ranks
    chips = ranks // 2
    chunk = min(256, rows)
    chunks = rows // chunk
    f32 = jnp.float32
    dma = pltpu.SemaphoreType.DMA
    vmem = pl.BlockSpec(memory_space=pltpu.VMEM)
    smem = pl.BlockSpec(memory_space=pltpu.SMEM)
    return pl.pallas_call(
        functools.partial(kernel, sections, chips, chunk),
        out_shape=jax.ShapeDtypeStruct((1, rows, width), f32),
        in_specs=[vmem, vmem, smem, smem],
        out_specs=vmem,
        scratch_shapes=[
            pltpu.VMEM((2, tokens, width), f32),
            pltpu.VMEM((2, tokens, width), f32),
            pltpu.VMEM((2, chips, chunks, tokens, chunk), f32),
            pltpu.VMEM((2, chips, chunks, tokens, chunk), f32),
            pltpu.VMEM((2, 2 * tokens, width), jnp.bfloat16),
            pltpu.VMEM((2, chips - 1, chunks, chunk, width), f32),
            pltpu.VMEM((2, chips - 1, chunks, chunk, width), f32),
            pltpu.VMEM((chunks, chunk, width), f32),
            pltpu.VMEM((chunks, chunk, width), f32),
            dma((2,)), dma((2,)),
            dma((2, chips, chunks)), dma((2, chips, chunks)),
            dma((2, chips - 1, chunks)), dma((2, chips - 1, chunks)),
            dma((chunks,)), dma((chunks,)),
        ],
        compiler_params=pltpu.CompilerParams(
            collective_id=0, has_side_effects=True, vmem_limit_bytes=40 * 2**20),
        cost_estimate=pl.CostEstimate(
            flops=8 * tokens * rows * chips * width,
            bytes_accessed=4 * tokens * rows * ranks + 4 * rows * width, transcendentals=0),
    )(hidden, grad_out, live_cols, tok_count)


def solution(mesh):
    in_specs = (
        P(None, "section", "fsdp", None),
        P(None, "section", "fsdp", None),
        P(),
        P(None, "fsdp"),
    )
    out_specs = P("section", "fsdp", None)
    body = functools.partial(on_device, mesh.shape["section"], mesh.shape["fsdp"])
    return jax.shard_map(
        body, mesh=mesh, in_specs=in_specs, out_specs=out_specs, check_vma=False
    )
```

```python
import functools

import jax
import jax.numpy as jnp
from jax import lax
from jax.experimental import pallas as pl
from jax.experimental.pallas import tpu as pltpu
from jax.sharding import PartitionSpec as P

MESH = pl.DeviceIdType.MESH


def kernel(
    sections, chips, chunk, hidden_hbm, grads_hbm, live_hbm, tok_hbm, out,
    hidden, grads, live_cols, tok_count, total, fetch_sem, out_sem,
    mask_send, mask_recv, in_send, in_recv, own_mask, part_send, part_recv, far_send, far_recv,
    mask_ss, mask_rs, in_ss, in_rs, part_ss, part_rs, far_ss, far_rs,
):
    tokens, width = hidden.shape[1], hidden.shape[2]
    rows = out.shape[1]
    chunks = rows // chunk
    sec = lax.axis_index("section")
    rank = lax.axis_index("fsdp")
    chip, core = rank // 2, rank % 2
    sibling = {"section": sec, "fsdp": chip * 2 + (1 - core)}
    mirrored = {"section": sections - 1 - sec, "fsdp": rank}

    def peer(j):
        return {"section": sec, "fsdp": lax.rem(chip + j, chips) * 2 + core}

    barrier = pltpu.get_barrier_semaphore()
    for target in [sibling, mirrored] + [peer(j) for j in range(1, chips)]:
        pl.semaphore_signal(barrier, inc=1, device_id=target, device_id_type=MESH)

    def columns(j, c, k):
        block = lax.rem(chip + j, chips) * 2 + c
        return pl.ds(pl.multiple_of(block * rows + k * chunk, chunk), chunk)

    def mask_copy(d):
        return pltpu.make_async_remote_copy(
            mask_send.at[d], mask_recv.at[d], mask_ss.at[d], mask_rs.at[d],
            device_id=sibling, device_id_type=MESH)

    def in_copy(d, j, k):
        return pltpu.make_async_remote_copy(
            in_send.at[d, j, k], in_recv.at[d, j, k], in_ss.at[d, j, k], in_rs.at[d, j, k],
            device_id=sibling, device_id_type=MESH)

    def part_copy(d, j, k):
        return pltpu.make_async_remote_copy(
            part_send.at[d, j - 1, k], part_recv.at[d, j - 1, k],
            part_ss.at[d, j - 1, k], part_rs.at[d, j - 1, k],
            device_id=peer(j), device_id_type=MESH)

    def far_copy(k):
        return pltpu.make_async_remote_copy(
            far_send.at[k], far_recv.at[k], far_ss.at[k], far_rs.at[k],
            device_id=mirrored, device_id_type=MESH)

    def fetch(d):
        return (
            pltpu.make_async_copy(hidden_hbm.at[d, 0], hidden.at[d], fetch_sem.at[d]),
            pltpu.make_async_copy(grads_hbm.at[d, 0], grads.at[d], fetch_sem.at[2 + d]))

    counts = (
        pltpu.make_async_copy(live_hbm, live_cols, fetch_sem.at[4]),
        pltpu.make_async_copy(tok_hbm, tok_count, fetch_sem.at[5]))
    for copy in counts + fetch(1) + fetch(0):
        copy.start()
    for copy in counts:
        copy.wait()
    positions = lax.broadcasted_iota(jnp.int32, (tokens, width), 0)
    column_ids = lax.broadcasted_iota(jnp.int32, (tokens, width), 1)
    live = (live_cols[sec], live_cols[sections - 1 - sec])
    order = [(k, j) for k in range(chunks) for j in list(range(1, chips)) + [0]]

    def stage(d):
        for copy in fetch(d):
            copy.wait()
        keep = (positions < tok_count[d]) & (column_ids < live[d])
        masked = jnp.where(keep, hidden[d].astype(jnp.float32), 0.0)
        mask_send[d] = masked
        own_mask[d, :tokens] = masked.astype(jnp.bfloat16)
        if d:
            pl.semaphore_wait(barrier, chips + 1)
        mask_copy(d).start()
        for k, j in order:
            in_send[d, j, k] = grads[d, :, columns(j, 1 - core, k)].astype(jnp.float32)
            in_copy(d, j, k).start()

    def take_mask(d):
        mask_copy(d).wait_recv()
        own_mask[d, tokens:] = mask_recv[d].astype(jnp.bfloat16)

    def partial(d, j, k):
        in_copy(d, j, k).wait_recv()
        both = jnp.concatenate(
            [grads[d, :, columns(j, core, k)], in_recv[d, j, k].astype(jnp.bfloat16)], axis=0)
        return lax.dot_general(
            both, own_mask[d], (((0,), (0,)), ((), ())), preferred_element_type=jnp.float32)

    def send_parts(d, k):
        for j in range(1, chips):
            part_send[d, j - 1, k] = partial(d, j, k)
            part_copy(d, j, k).start()

    def forward(k):
        reduced = far_send[k]
        for j in range(1, chips):
            part_copy(1, j, k).wait_recv()
            reduced = reduced + part_recv[1, j - 1, k]
        far_send[k] = reduced
        far_copy(k).start()

    lag = min(3, chunks)
    stage(1)
    take_mask(1)
    for k in range(lag):
        send_parts(1, k)
    for k in range(lag):
        far_send[k] = partial(1, 0, k)
    stage(0)
    for k in range(chunks):
        forward(k)
        if k + lag < chunks:
            send_parts(1, k + lag)
            far_send[k + lag] = partial(1, 0, k + lag)
        else:
            if k + lag == chunks:
                take_mask(0)
            send_parts(0, k + lag - chunks)
    for k in range(lag, chunks):
        send_parts(0, k)
    for k in range(chunks):
        total[k] = partial(0, 0, k)
    for k in range(chunks):
        reduced = total[k]
        for j in range(1, chips):
            part_copy(0, j, k).wait_recv()
            reduced = reduced + part_recv[0, j - 1, k]
        total[k] = reduced
    for d in (1, 0):
        mask_copy(d).wait_send()
        for k, j in order:
            in_copy(d, j, k).wait_send()
            if j:
                part_copy(d, j, k).wait_send()

    def store(k):
        return pltpu.make_async_copy(
            total.at[k], out.at[0, k * chunk:(k + 1) * chunk], out_sem.at[k])

    for k in range(chunks):
        far_copy(k).wait_recv()
        total[k] += far_recv[k]
        store(k).start()
    for k in range(chunks):
        far_copy(k).wait_send()
        store(k).wait()


def on_device(sections, ranks, hidden, grad_out, live_cols, tok_count):
    tokens, width = hidden.shape[2], hidden.shape[3]
    rows = grad_out.shape[3] // ranks
    chips = ranks // 2
    chunk = min(128, rows)
    chunks = rows // chunk
    f32 = jnp.float32
    dma = pltpu.SemaphoreType.DMA
    hbm = pl.BlockSpec(memory_space=pltpu.HBM)
    return pl.pallas_call(
        functools.partial(kernel, sections, chips, chunk),
        out_shape=jax.ShapeDtypeStruct((1, rows, width), f32),
        in_specs=[hbm] * 4,
        out_specs=hbm,
        scratch_shapes=[
            pltpu.VMEM((2, tokens, width), jnp.bfloat16),
            pltpu.VMEM((2, tokens, grad_out.shape[3]), jnp.bfloat16),
            pltpu.SMEM(live_cols.shape, jnp.int32),
            pltpu.SMEM((2,), jnp.int32),
            pltpu.VMEM((chunks, chunk, width), f32),
            dma((6,)), dma((chunks,)),
            pltpu.VMEM((2, tokens, width), f32),
            pltpu.VMEM((2, tokens, width), f32),
            pltpu.VMEM((2, chips, chunks, tokens, chunk), f32),
            pltpu.VMEM((2, chips, chunks, tokens, chunk), f32),
            pltpu.VMEM((2, 2 * tokens, width), jnp.bfloat16),
            pltpu.VMEM((2, chips - 1, chunks, chunk, width), f32),
            pltpu.VMEM((2, chips - 1, chunks, chunk, width), f32),
            pltpu.VMEM((chunks, chunk, width), f32),
            pltpu.VMEM((chunks, chunk, width), f32),
            dma((2,)), dma((2,)),
            dma((2, chips, chunks)), dma((2, chips, chunks)),
            dma((2, chips - 1, chunks)), dma((2, chips - 1, chunks)),
            dma((chunks,)), dma((chunks,)),
        ],
        compiler_params=pltpu.CompilerParams(
            collective_id=0, has_side_effects=True, vmem_limit_bytes=48 * 2**20),
        cost_estimate=pl.CostEstimate(
            flops=8 * tokens * rows * chips * width,
            bytes_accessed=4 * tokens * rows * ranks + 4 * rows * width, transcendentals=0),
    )(*(pltpu.with_memory_space_constraint(a, pltpu.HBM) for a in (hidden, grad_out, live_cols, tok_count.reshape(2))))


def solution(mesh):
    in_specs = (
        P(None, "section", "fsdp", None),
        P(None, "section", "fsdp", None),
        P(),
        P(None, "fsdp"),
    )
    out_specs = P("section", "fsdp", None)
    body = functools.partial(on_device, mesh.shape["section"], mesh.shape["fsdp"])
    return jax.shard_map(
        body, mesh=mesh, in_specs=in_specs, out_specs=out_specs, check_vma=False
    )
```

```python
import functools

import jax
import jax.numpy as jnp
from jax import lax
from jax.experimental import pallas as pl
from jax.experimental.pallas import tpu as pltpu
from jax.sharding import PartitionSpec as P

MESH = pl.DeviceIdType.MESH


def kernel(
    sections, chips, chunk, hidden_hbm, grads_hbm, live_hbm, tok_hbm, out,
    hidden, grads, live_cols, tok_count, total, fetch_sem,
    mask_send, mask_recv, in_send, in_recv, own_mask, part_send, part_recv, far_send, far_recv,
    mask_ss, mask_rs, in_ss, in_rs, part_ss, part_rs, far_ss, far_rs,
):
    tokens, width = hidden.shape[1], hidden.shape[2]
    rows = out.shape[1]
    chunks = rows // chunk
    sec = lax.axis_index("section")
    rank = lax.axis_index("fsdp")
    chip, core = rank // 2, rank % 2
    sibling = {"section": sec, "fsdp": chip * 2 + (1 - core)}
    mirrored = {"section": sections - 1 - sec, "fsdp": rank}

    def peer(j):
        return {"section": sec, "fsdp": lax.rem(chip + j, chips) * 2 + core}

    barrier = pltpu.get_barrier_semaphore()
    for target in [sibling, mirrored] + [peer(j) for j in range(1, chips)]:
        pl.semaphore_signal(barrier, inc=1, device_id=target, device_id_type=MESH)

    def columns(j, c, k):
        block = lax.rem(chip + j, chips) * 2 + c
        return pl.ds(pl.multiple_of(block * rows + k * chunk, chunk), chunk)

    def mask_copy(d):
        return pltpu.make_async_remote_copy(
            mask_send.at[d], mask_recv.at[d], mask_ss.at[d], mask_rs.at[d],
            device_id=sibling, device_id_type=MESH)

    def in_copy(d, j, k):
        return pltpu.make_async_remote_copy(
            in_send.at[d, j, k], in_recv.at[d, j, k], in_ss.at[d, j, k], in_rs.at[d, j, k],
            device_id=sibling, device_id_type=MESH)

    def part_copy(d, j, k):
        return pltpu.make_async_remote_copy(
            part_send.at[d, j - 1, k], part_recv.at[d, j - 1, k],
            part_ss.at[d, j - 1, k], part_rs.at[d, j - 1, k],
            device_id=peer(j), device_id_type=MESH)

    def far_copy(k):
        return pltpu.make_async_remote_copy(
            far_send.at[k], far_recv.at[k], far_ss.at[k], far_rs.at[k],
            device_id=mirrored, device_id_type=MESH)

    def fetch(d):
        return (
            pltpu.make_async_copy(hidden_hbm.at[d, 0], hidden.at[d], fetch_sem.at[d]),
            pltpu.make_async_copy(grads_hbm.at[d, 0], grads.at[d], fetch_sem.at[2 + d]))

    counts = (
        pltpu.make_async_copy(live_hbm, live_cols, fetch_sem.at[4]),
        pltpu.make_async_copy(tok_hbm, tok_count, fetch_sem.at[5]))
    for copy in counts + fetch(1) + fetch(0):
        copy.start()
    for copy in counts:
        copy.wait()
    positions = lax.broadcasted_iota(jnp.int32, (tokens, width), 0)
    column_ids = lax.broadcasted_iota(jnp.int32, (tokens, width), 1)
    live = (live_cols[sec], live_cols[sections - 1 - sec])
    order = [(k, j) for k in range(chunks) for j in list(range(1, chips)) + [0]]

    def stage(d):
        for copy in fetch(d):
            copy.wait()
        keep = (positions < tok_count[d]) & (column_ids < live[d])
        masked = jnp.where(keep, hidden[d].astype(jnp.float32), 0.0)
        mask_send[d] = masked
        own_mask[d, :tokens] = masked.astype(jnp.bfloat16)
        if d:
            pl.semaphore_wait(barrier, chips + 1)
        mask_copy(d).start()

    def spread(d, blocks):
        for k, j in blocks:
            in_send[d, j, k] = grads[d, :, columns(j, 1 - core, k)].astype(jnp.float32)
            in_copy(d, j, k).start()

    def take_mask(d):
        mask_copy(d).wait_recv()
        own_mask[d, tokens:] = mask_recv[d].astype(jnp.bfloat16)

    def partial(d, j, k):
        in_copy(d, j, k).wait_recv()
        both = jnp.concatenate(
            [grads[d, :, columns(j, core, k)], in_recv[d, j, k].astype(jnp.bfloat16)], axis=0)
        return lax.dot_general(
            both, own_mask[d], (((0,), (0,)), ((), ())), preferred_element_type=jnp.float32)

    def send_parts(d, k):
        for j in range(1, chips):
            part_send[d, j - 1, k] = partial(d, j, k)
            part_copy(d, j, k).start()

    def forward(k):
        reduced = far_send[k]
        for j in range(1, chips):
            part_copy(1, j, k).wait_recv()
            reduced = reduced + part_recv[1, j - 1, k]
        far_send[k] = reduced
        far_copy(k).start()

    lag = min(2, chunks)
    stage(1)
    spread(1, order[:chips])
    spread(1, order[chips:2 * chips])
    take_mask(1)
    send_parts(1, 0)
    spread(1, order[2 * chips:])
    for k in range(1, lag):
        send_parts(1, k)
    for k in range(lag):
        far_send[k] = partial(1, 0, k)
    stage(0)
    spread(0, order)
    for k in range(chunks):
        forward(k)
        if k + lag < chunks:
            send_parts(1, k + lag)
            far_send[k + lag] = partial(1, 0, k + lag)
        else:
            if k + lag == chunks:
                take_mask(0)
            send_parts(0, k + lag - chunks)
    for k in range(lag, chunks):
        send_parts(0, k)
    for k in range(chunks):
        total[k] = partial(0, 0, k)
    for k in range(chunks):
        reduced = total[k]
        for j in range(1, chips):
            part_copy(0, j, k).wait_recv()
            reduced = reduced + part_recv[0, j - 1, k]
        total[k] = reduced
    for d in (1, 0):
        mask_copy(d).wait_send()
        for k, j in order:
            in_copy(d, j, k).wait_send()
            if j:
                part_copy(d, j, k).wait_send()

    for k in range(chunks):
        far_copy(k).wait_recv()
        out[0, k * chunk:(k + 1) * chunk] = total[k] + far_recv[k]
    for k in range(chunks):
        far_copy(k).wait_send()


def on_device(sections, ranks, hidden, grad_out, live_cols, tok_count):
    tokens, width = hidden.shape[2], hidden.shape[3]
    rows = grad_out.shape[3] // ranks
    chips = ranks // 2
    chunk = min(128, rows)
    chunks = rows // chunk
    f32 = jnp.float32
    dma = pltpu.SemaphoreType.DMA
    hbm = pl.BlockSpec(memory_space=pltpu.HBM)
    return pl.pallas_call(
        functools.partial(kernel, sections, chips, chunk),
        out_shape=jax.ShapeDtypeStruct((1, rows, width), f32),
        in_specs=[hbm] * 4,
        out_specs=pl.BlockSpec(memory_space=pltpu.VMEM),
        scratch_shapes=[
            pltpu.VMEM((2, tokens, width), jnp.bfloat16),
            pltpu.VMEM((2, tokens, grad_out.shape[3]), jnp.bfloat16),
            pltpu.SMEM(live_cols.shape, jnp.int32),
            pltpu.SMEM((2,), jnp.int32),
            pltpu.VMEM((chunks, chunk, width), f32),
            dma((6,)),
            pltpu.VMEM((2, tokens, width), f32),
            pltpu.VMEM((2, tokens, width), f32),
            pltpu.VMEM((2, chips, chunks, tokens, chunk), f32),
            pltpu.VMEM((2, chips, chunks, tokens, chunk), f32),
            pltpu.VMEM((2, 2 * tokens, width), jnp.bfloat16),
            pltpu.VMEM((2, chips - 1, chunks, chunk, width), f32),
            pltpu.VMEM((2, chips - 1, chunks, chunk, width), f32),
            pltpu.VMEM((chunks, chunk, width), f32),
            pltpu.VMEM((chunks, chunk, width), f32),
            dma((2,)), dma((2,)),
            dma((2, chips, chunks)), dma((2, chips, chunks)),
            dma((2, chips - 1, chunks)), dma((2, chips - 1, chunks)),
            dma((chunks,)), dma((chunks,)),
        ],
        compiler_params=pltpu.CompilerParams(
            collective_id=0, has_side_effects=True, vmem_limit_bytes=48 * 2**20),
        cost_estimate=pl.CostEstimate(
            flops=8 * tokens * rows * chips * width,
            bytes_accessed=4 * tokens * rows * ranks + 4 * rows * width, transcendentals=0),
    )(*(pltpu.with_memory_space_constraint(a, pltpu.HBM) for a in (hidden, grad_out, live_cols, tok_count.reshape(2))))


def solution(mesh):
    in_specs = (
        P(None, "section", "fsdp", None),
        P(None, "section", "fsdp", None),
        P(),
        P(None, "fsdp"),
    )
    out_specs = P("section", "fsdp", None)
    body = functools.partial(on_device, mesh.shape["section"], mesh.shape["fsdp"])
    return jax.shard_map(
        body, mesh=mesh, in_specs=in_specs, out_specs=out_specs, check_vma=False
    )
```

```python
import functools

import jax
import jax.numpy as jnp
from jax import lax
from jax.experimental import pallas as pl
from jax.experimental.pallas import tpu as pltpu
from jax.sharding import PartitionSpec as P

MESH = pl.DeviceIdType.MESH


def kernel(
    sections, chips, chunk, hidden_hbm, grads_hbm, live_hbm, tok_hbm, out,
    hidden, grads, live_cols, tok_count, total, fetch_sem,
    mask_send, mask_recv, in_send, in_recv, own_mask, part_send, part_recv, far_send, far_recv,
    mask_ss, mask_rs, in_ss, in_rs, part_ss, part_rs, far_ss, far_rs,
):
    tokens, width = hidden.shape[1], hidden.shape[2]
    rows = out.shape[1]
    chunks = rows // chunk
    sec = lax.axis_index("section")
    rank = lax.axis_index("fsdp")
    chip, core = rank // 2, rank % 2
    sibling = {"section": sec, "fsdp": chip * 2 + (1 - core)}
    mirrored = {"section": sections - 1 - sec, "fsdp": rank}

    def peer(j):
        return {"section": sec, "fsdp": lax.rem(chip + j, chips) * 2 + core}

    barrier = pltpu.get_barrier_semaphore()
    for target in [sibling, mirrored] + [peer(j) for j in range(1, chips)]:
        pl.semaphore_signal(barrier, inc=1, device_id=target, device_id_type=MESH)

    def columns(j, c, k):
        block = lax.rem(chip + j, chips) * 2 + c
        return pl.ds(pl.multiple_of(block * rows + k * chunk, chunk), chunk)

    def mask_copy(d):
        return pltpu.make_async_remote_copy(
            mask_send.at[d], mask_recv.at[d], mask_ss.at[d], mask_rs.at[d],
            device_id=sibling, device_id_type=MESH)

    def in_copy(d, j, k):
        return pltpu.make_async_remote_copy(
            in_send.at[d, j, k], in_recv.at[d, j, k], in_ss.at[d, j, k], in_rs.at[d, j, k],
            device_id=sibling, device_id_type=MESH)

    def part_copy(d, j, k):
        return pltpu.make_async_remote_copy(
            part_send.at[d, j - 1, k], part_recv.at[d, j - 1, k],
            part_ss.at[d, j - 1, k], part_rs.at[d, j - 1, k],
            device_id=peer(j), device_id_type=MESH)

    def far_copy(k):
        return pltpu.make_async_remote_copy(
            far_send.at[k], far_recv.at[k], far_ss.at[k], far_rs.at[k],
            device_id=mirrored, device_id_type=MESH)

    def fetch(d):
        return (
            pltpu.make_async_copy(hidden_hbm.at[d, 0], hidden.at[d], fetch_sem.at[d]),
            pltpu.make_async_copy(grads_hbm.at[d, 0], grads.at[d], fetch_sem.at[2 + d]))

    counts = (
        pltpu.make_async_copy(live_hbm, live_cols, fetch_sem.at[4]),
        pltpu.make_async_copy(tok_hbm, tok_count, fetch_sem.at[5]))
    for copy in counts + fetch(1) + fetch(0):
        copy.start()
    for copy in counts:
        copy.wait()
    positions = lax.broadcasted_iota(jnp.int32, (tokens, width), 0)
    column_ids = lax.broadcasted_iota(jnp.int32, (tokens, width), 1)
    live = (live_cols[sec], live_cols[sections - 1 - sec])
    order = [(k, j) for k in range(chunks) for j in list(range(1, chips)) + [0]]

    def stage(d):
        for copy in fetch(d):
            copy.wait()
        keep = (positions < tok_count[d]) & (column_ids < live[d])
        masked = jnp.where(keep, hidden[d].astype(jnp.float32), 0.0)
        mask_send[d] = masked
        own_mask[d, :tokens] = masked.astype(jnp.bfloat16)
        if d:
            pl.semaphore_wait(barrier, chips + 1)
        mask_copy(d).start()

    def spread(d, blocks):
        for k, j in blocks:
            in_send[d, j, k] = grads[d, :, columns(j, 1 - core, k)].astype(jnp.float32)
            in_copy(d, j, k).start()

    def take_mask(d):
        mask_copy(d).wait_recv()
        own_mask[d, tokens:] = mask_recv[d].astype(jnp.bfloat16)

    def partial(d, j, k):
        in_copy(d, j, k).wait_recv()
        both = jnp.concatenate(
            [grads[d, :, columns(j, core, k)], in_recv[d, j, k].astype(jnp.bfloat16)], axis=0)
        return lax.dot_general(
            both, own_mask[d], (((0,), (0,)), ((), ())), preferred_element_type=jnp.float32)

    def send_parts(d, k):
        for j in range(1, chips):
            part_send[d, j - 1, k] = partial(d, j, k)
            part_copy(d, j, k).start()

    def forward(k):
        reduced = far_send[k]
        for j in range(1, chips):
            part_copy(1, j, k).wait_recv()
            reduced = reduced + part_recv[1, j - 1, k]
        far_send[k] = reduced
        far_copy(k).start()

    lag = min(2, chunks)
    stage(1)
    spread(1, order[:chips])
    spread(1, order[chips:2 * chips])
    take_mask(1)
    send_parts(1, 0)
    spread(1, order[2 * chips:])
    for k in range(1, lag):
        send_parts(1, k)
    far_send[0] = partial(1, 0, 0)
    for k in range(chunks):
        if k:
            far_send[k] = partial(1, 0, k)
        forward(k)
        if k == 0:
            stage(0)
            spread(0, order)
        if k + lag < chunks:
            send_parts(1, k + lag)
        else:
            if k + lag == chunks:
                take_mask(0)
            send_parts(0, k + lag - chunks)
    for k in range(lag, chunks):
        send_parts(0, k)
    for k in range(chunks):
        total[k] = partial(0, 0, k)
    for k in range(chunks):
        reduced = total[k]
        for j in range(1, chips):
            part_copy(0, j, k).wait_recv()
            reduced = reduced + part_recv[0, j - 1, k]
        total[k] = reduced
    for d in (1, 0):
        mask_copy(d).wait_send()
        for k, j in order:
            in_copy(d, j, k).wait_send()
            if j:
                part_copy(d, j, k).wait_send()

    for k in range(chunks):
        far_copy(k).wait_recv()
        out[0, k * chunk:(k + 1) * chunk] = total[k] + far_recv[k]
    for k in range(chunks):
        far_copy(k).wait_send()


def on_device(sections, ranks, hidden, grad_out, live_cols, tok_count):
    tokens, width = hidden.shape[2], hidden.shape[3]
    rows = grad_out.shape[3] // ranks
    chips = ranks // 2
    chunk = min(128, rows)
    chunks = rows // chunk
    f32 = jnp.float32
    dma = pltpu.SemaphoreType.DMA
    hbm = pl.BlockSpec(memory_space=pltpu.HBM)
    return pl.pallas_call(
        functools.partial(kernel, sections, chips, chunk),
        out_shape=jax.ShapeDtypeStruct((1, rows, width), f32),
        in_specs=[hbm] * 4,
        out_specs=pl.BlockSpec(memory_space=pltpu.VMEM),
        scratch_shapes=[
            pltpu.VMEM((2, tokens, width), jnp.bfloat16),
            pltpu.VMEM((2, tokens, grad_out.shape[3]), jnp.bfloat16),
            pltpu.SMEM(live_cols.shape, jnp.int32),
            pltpu.SMEM((2,), jnp.int32),
            pltpu.VMEM((chunks, chunk, width), f32),
            dma((6,)),
            pltpu.VMEM((2, tokens, width), f32),
            pltpu.VMEM((2, tokens, width), f32),
            pltpu.VMEM((2, chips, chunks, tokens, chunk), f32),
            pltpu.VMEM((2, chips, chunks, tokens, chunk), f32),
            pltpu.VMEM((2, 2 * tokens, width), jnp.bfloat16),
            pltpu.VMEM((2, chips - 1, chunks, chunk, width), f32),
            pltpu.VMEM((2, chips - 1, chunks, chunk, width), f32),
            pltpu.VMEM((chunks, chunk, width), f32),
            pltpu.VMEM((chunks, chunk, width), f32),
            dma((2,)), dma((2,)),
            dma((2, chips, chunks)), dma((2, chips, chunks)),
            dma((2, chips - 1, chunks)), dma((2, chips - 1, chunks)),
            dma((chunks,)), dma((chunks,)),
        ],
        compiler_params=pltpu.CompilerParams(
            collective_id=0, has_side_effects=True, vmem_limit_bytes=48 * 2**20),
        cost_estimate=pl.CostEstimate(
            flops=8 * tokens * rows * chips * width,
            bytes_accessed=4 * tokens * rows * ranks + 4 * rows * width, transcendentals=0),
    )(*(pltpu.with_memory_space_constraint(a, pltpu.HBM) for a in (hidden, grad_out, live_cols, tok_count.reshape(2))))


def solution(mesh):
    in_specs = (
        P(None, "section", "fsdp", None),
        P(None, "section", "fsdp", None),
        P(),
        P(None, "fsdp"),
    )
    out_specs = P("section", "fsdp", None)
    body = functools.partial(on_device, mesh.shape["section"], mesh.shape["fsdp"])
    return jax.shard_map(
        body, mesh=mesh, in_specs=in_specs, out_specs=out_specs, check_vma=False
    )
```
